256 devices in a mesh: hid: 8 (over y, core), voc: 32 (over x, z).
Axes of the slice: x: 4, y: 4, z: 8, core: 2. Of those that a mesh axis runs over, the one named last changes fastest.
Arguments:
- hidden: bfloat16 [1024, 7168], P(None, 'hid'), may hold values from -310 to 310
- target: bfloat16 [1024, 64640], P(None, 'voc'), may hold values from -30 to 360
- head: bfloat16 [7168, 64640], P('hid', 'voc'), may hold values from -0.0625 to 0.0625
- cotangent: float32 [1024], replicated, may hold values from 30 to 300
Outputs:
- hidden_grad: bfloat16 [1024, 7168], P('voc', 'hid')
- head_grad: bfloat16 [7168, 64640], P('hid', 'voc')
- divergence: float32 [1024], P('hid')
The draws below stay inside these ranges and needn't reach their ends.
All inputs are finite; a program needn't handle non-finite values.
Results may differ from the reference program's by a relative error of at most 0.0057.
Values may be sent and summed in bfloat16 or wider, within the bound.
A program may use at most 128 MiB of HBM per device.

```python
import math
import jax
import jax.numpy as jnp

D = 7168
V = 64640
ROWS = 1024


def draw_hidden(key, part):
    key = jax.random.fold_in(key, 1)
    values = jnp.clip(jax.random.normal(key, (ROWS, D), jnp.float32), -6.0, 6.0)
    return values.astype(jnp.bfloat16)


def draw_target(key, part):
    key = jax.random.fold_in(key, 2)
    values = 3.0 * jnp.clip(jax.random.normal(key, (ROWS, V), jnp.float32), -6.0, 6.0)
    return values.astype(jnp.bfloat16)


def steps_of(key, extent, split, smallest, largest):
    def one(axis_at, parts):
        steps = jax.random.uniform(jax.random.fold_in(jax.random.fold_in(key, 6), axis_at), (parts,), jnp.float32, smallest / len(split), largest / len(split))
        return jnp.repeat(jnp.exp(steps), extent[axis_at] // parts).reshape((-1,) + (1,) * (len(extent) - axis_at - 1))

    level = one(*split[0])
    for cut in split[1:]:
        level = level * one(*cut)
    return level


def gaussian(rng, shape, deviation, most, shards=(), kind=jnp.bfloat16):
    level = steps_of(rng, shape, shards, -0.22, 0.18) if shards else 1.0
    result = jax.random.normal(rng, shape, jnp.float32) * deviation * level
    return jnp.minimum(jnp.maximum(result, -most), most).astype(kind)


def setup_inputs(seed: int = 0) -> dict:
    seeds = jax.random.split(jax.random.key(seed), 5)
    return {
        "hidden": draw_hidden(jax.random.fold_in(seeds[4], 71), 0),
        "target": draw_target(jax.random.fold_in(seeds[4], 71), 0),
        "head": gaussian(seeds[2], (D, V), D ** -0.5, 0.0625, ((0, 8), (1, 32))),
        "cotangent": jnp.clip(jnp.exp(jax.random.uniform(seeds[3], (ROWS,), jnp.float32, math.log(30.0), math.log(300.0))), 30.0, 300.0),
    }


def reference(hidden, target, head, cotangent):
    draft = jnp.dot(hidden, head, preferred_element_type=jnp.float32)
    log_q = jax.nn.log_softmax(draft, axis=-1)
    log_p = jax.nn.log_softmax(target.astype(jnp.float32), axis=-1)
    probs_p = jnp.exp(log_p)
    probs_q = jnp.exp(log_q)
    divergence = jnp.sum(probs_p * (log_p - log_q), axis=-1)
    grad = (cotangent[:, None] * (probs_q - probs_p)).astype(jnp.bfloat16)
    hidden_grad = jnp.dot(grad, head.T, preferred_element_type=jnp.float32).astype(jnp.bfloat16)
    head_grad = jnp.dot(hidden.T, grad, preferred_element_type=jnp.float32).astype(jnp.bfloat16)
    return hidden_grad, head_grad, divergence
```

```python
import jax
import jax.numpy as jnp
from jax import lax
from jax.experimental import pallas as pl
from jax.experimental.pallas import tpu as pltpu
from jax.sharding import PartitionSpec as P

MESH = pl.DeviceIdType.MESH
F32, BF16 = jnp.float32, jnp.bfloat16
CHUNKS = ((0,), (2, 4), (6, 1), (3, 5), (7,))
N = len(CHUNKS)
SIZE = [16 * len(groups) for groups in CHUNKS]
BASE = [sum(SIZE[:c]) for c in range(N)]
WIDE = 256
ORDER = (
    "M0", "M1", "A0", "A1", "T0", "M2", "B0", "B1", "A2", "L0", "X0", "M3", "L1", "B2", "G0", "M4", "X1", "A3",
    "L2", "F0", "X2", "G1", "H0", "B3", "K0", "F1", "G2", "L3", "R0", "H1", "A4", "K1", "X3", "F2", "Z0", "B4",
    "G3", "H2", "R1", "L4", "K2", "X4", "F3", "Z1", "R2", "H3", "G4", "K3", "F4", "Z2", "R3", "H4", "O1", "K4",
    "Z3", "O0", "R4", "O2", "Z4", "W2", "W1", "W3", "O3", "W0", "O4",
)


def place(*refs):
    sem = refs[-1]
    copies = []
    for src, dst in zip(refs[:3], refs[3:6]):
        step = -(-src.shape[0] // 64) * 16
        for i in range(0, src.shape[0], step):
            span = pl.ds(i, min(step, src.shape[0] - i))
            copies.append(pltpu.make_async_copy(src.at[span], dst.at[span], sem.at[len(copies)]))
    for copy in copies:
        copy.start()
    for copy in copies:
        copy.wait()


def kernel(
    hidden, target, head, cot, wgrad, hgrad, div,
    tgt_in, tgt_s, head_s, part, sib_r, ya_r, yb_r, ed, et, loc, turn, stx, stz, cotcol, divcol,
    grad, hgp, xa_r, xb_r, zr, load_sem, send_sem, recv_sem, *hid_s,
):
    hid, voc = lax.axis_index("hid"), lax.axis_index("voc")
    y, core = hid // 2, hid % 2
    x, z = voc // 8, voc % 8
    vocab, depth = head.shape
    padded = part.shape[1]
    halves = (pl.ds(0, padded // 2), pl.ds(padded // 2, padded // 2))

    def at(yy=y, cc=core, xx=x, zz=z):
        return {"hid": yy * 2 + cc, "voc": xx * 8 + zz}

    yp, ym, yo = (y + 1) % 4, (y + 3) % 4, (y + 2) % 4
    xp, xm, xo = (x + 1) % 4, (x + 3) % 4, (x + 2) % 4
    sibling = at(cc=1 - core)
    partners = [sibling, at(yy=yp), at(yy=ym)]
    partners += [at(xx=(x + d) % 4) for d in (1, 2, 3)]
    partners += [at(zz=(z + d) % 8) for d in range(1, 8)]

    barrier = pltpu.get_barrier_semaphore()
    for partner in partners:
        pl.semaphore_signal(barrier, inc=1, device_id=partner, device_id_type=MESH)

    loads = {}

    def load(name, src, dst):
        copy = pltpu.make_async_copy(src, dst, load_sem.at[sum(map(len, loads.values()))])
        copy.start()
        loads.setdefault(name, []).append(copy)

    def load_hidden(c):
        for i, g in enumerate(CHUNKS[c]):
            for k in (0, 1):
                load(c, hidden.at[:, k, g], hid_s[c].at[k, :, i])

    def loaded(name):
        for copy in loads[name]:
            copy.wait()

    load_hidden(0)
    for i in range(0, vocab, 512):
        span = pl.ds(i, min(512, vocab - i))
        load("head", head.at[span], head_s.at[span])
    load("target", target.at[:, pl.ds(pl.multiple_of(hid * 128, 128), 128)], tgt_in)
    load("cot", cot, cotcol.at[pl.ds(0, 8)])
    for c in range(1, N):
        load_hidden(c)

    copies = {}

    def remote(name, src, dst, device):
        n = len(copies)
        copy = pltpu.make_async_remote_copy(
            src_ref=src, dst_ref=dst, send_sem=send_sem.at[n], recv_sem=recv_sem.at[n],
            device_id=device, device_id_type=MESH,
        )
        copies[name] = copy
        return copy

    def send(name, src, dst, device):
        remote(name, src, dst, device).start()

    def arrived(name):
        copies[name].wait_recv()

    def span(base, count):
        return pl.ds(base if isinstance(base, int) else pl.multiple_of(base, 16), count)

    def rows(c, yy, cc=core):
        return span(8 * BASE[c] + cc * 4 * SIZE[c] + yy * SIZE[c], SIZE[c])

    def chunk(c):
        return pl.ds(BASE[c], SIZE[c])

    def tiles(width):
        return [pl.ds(i, min(width, vocab - i)) for i in range(0, vocab, width)]

    def hidden_rows(c):
        return hid_s[c][...].reshape(8 * SIZE[c], depth)

    def stage_m(c):
        loaded(c)
        if c == 0:
            loaded("head")
        mine = pl.ds(8 * BASE[c], 8 * SIZE[c])
        for cols in tiles(512):
            part[mine, cols] = lax.dot_general(
                hidden_rows(c), head_s[cols, :], (((1,), (1,)), ((), ())), preferred_element_type=F32
            )
        part[mine, vocab:padded] = jnp.zeros((8 * SIZE[c], padded - vocab), F32)
        if c == 0:
            pl.semaphore_wait(barrier, len(partners))
        theirs = span(8 * BASE[c] + (1 - core) * 4 * SIZE[c], 4 * SIZE[c])
        send(f"sib{c}", part.at[theirs], sib_r.at[pl.ds(4 * BASE[c], 4 * SIZE[c])], sibling)

    def add_sibling(c, yy):
        mine = rows(c, yy)
        part[mine, :] = part[mine, :] + sib_r[span(4 * BASE[c] + yy * SIZE[c], SIZE[c]), :]

    def stage_a(c):
        low, high = halves
        arrived(f"sib{c}")
        add_sibling(c, yo)
        send(f"yap{c}", part.at[rows(c, yo), low], ya_r.at[0, chunk(c)], at(yy=yp))
        send(f"yam{c}", part.at[rows(c, yo), high], ya_r.at[1, chunk(c)], at(yy=ym))
        add_sibling(c, yp)
        send(f"ydp{c}", part.at[rows(c, yp), high], yb_r.at[0, chunk(c), high], at(yy=yp))
        add_sibling(c, ym)
        send(f"ydm{c}", part.at[rows(c, ym), low], yb_r.at[1, chunk(c), low], at(yy=ym))
        add_sibling(c, y)

    def stage_b(c):
        low, high = halves
        arrived(f"yap{c}")
        part[rows(c, yp), low] = part[rows(c, yp), low] + ya_r[0, chunk(c)]
        send(f"ybp{c}", part.at[rows(c, yp), low], yb_r.at[0, chunk(c), low], at(yy=yp))
        arrived(f"yam{c}")
        part[rows(c, ym), high] = part[rows(c, ym), high] + ya_r[1, chunk(c)]
        send(f"ybm{c}", part.at[rows(c, ym), high], yb_r.at[1, chunk(c), high], at(yy=ym))

    def own_rows(c):
        return [pl.ds(16 * g, 16) for g in CHUNKS[c]]

    def stage_t(_):
        turn[...] = jnp.zeros_like(turn)
        loaded("cot")
        cotcol[...] = jnp.broadcast_to(cotcol[pl.ds(hid, 1), :], (128, 128)).T
        loaded("target")
        tgt_s[...] = tgt_in[...].astype(F32).T

    def stage_l(c):
        for name in ("ydp", "ydm", "ybp", "ybm"):
            arrived(f"{name}{c}")
        d = part[rows(c, y), 0:vocab] + yb_r[0, chunk(c), 0:vocab] + yb_r[1, chunk(c), 0:vocab]
        t = jnp.concatenate([tgt_s[r, :] for r in own_rows(c)], axis=0)
        top_d = jnp.max(d, axis=1, keepdims=True)
        top_t = jnp.max(t, axis=1, keepdims=True)
        exp_d = jnp.exp(d - top_d)
        exp_t = jnp.exp(t - top_t)
        ed[chunk(c), :] = exp_d
        et[chunk(c), :] = exp_t
        sum_d = jnp.sum(exp_d, axis=1, keepdims=True)
        sum_t = jnp.sum(exp_t, axis=1, keepdims=True)
        numer = jnp.sum(exp_t * (t - d), axis=1, keepdims=True)
        lane = lax.broadcasted_iota(jnp.int32, (SIZE[c], 128), 1)
        both = jnp.zeros((SIZE[c], 128), F32)
        for k, column in enumerate((top_d, sum_d, top_t, sum_t, numer)):
            both = jnp.where(lane == k, column, both)
        loc[chunk(c), :] = both
        turn[pl.ds(0, SIZE[c]), :] = both
        stx[c, x] = turn[...].T[0:8, :]
        for d_ in (1, 2, 3):
            send(f"sx{d_}_{c}", stx.at[c, x], stx.at[c, x], at(xx=(x + d_) % 4))

    def merge(stats):
        top_d, top_t = stats[0][0:1], stats[0][2:3]
        for s in stats[1:]:
            top_d, top_t = jnp.maximum(top_d, s[0:1]), jnp.maximum(top_t, s[2:3])
        sum_d = sum_t = numer = jnp.zeros((1, 128), F32)
        for s in stats:
            scale_d, scale_t = jnp.exp(s[0:1] - top_d), jnp.exp(s[2:3] - top_t)
            sum_d, sum_t = sum_d + s[1:2] * scale_d, sum_t + s[3:4] * scale_t
            numer = numer + s[4:5] * scale_t
        return top_d, sum_d, top_t, sum_t, numer

    def stack(values):
        sub = lax.broadcasted_iota(jnp.int32, (8, 128), 0)
        both = jnp.zeros((8, 128), F32)
        for k, row in enumerate(values):
            both = jnp.where(sub == k, row, both)
        return both

    def stage_x(c):
        for d_ in (1, 2, 3):
            arrived(f"sx{d_}_{c}")
        stz[c, z] = stack(merge([stx[c, i] for i in range(4)]))
        for d_ in range(1, 8):
            send(f"sz{d_}_{c}", stz.at[c, z], stz.at[c, z], at(zz=(z + d_) % 8))

    def stage_g(c):
        for d_ in range(1, 8):
            arrived(f"sz{d_}_{c}")
        top_d, sum_d, top_t, sum_t, numer = merge([stz[c, i] for i in range(8)])
        norm_d, norm_t = top_d + jnp.log(sum_d), top_t + jnp.log(sum_t)
        divergence = numer / sum_t + norm_d - norm_t
        turn[pl.ds(0, 8), :] = stack((norm_d, norm_t, divergence))
        columns = turn[...].T[0 : SIZE[c], :]
        weight = jnp.concatenate([cotcol[r, :] for r in own_rows(c)], axis=0)[:, 0:1]
        for i, r in enumerate(own_rows(c)):
            divcol[r, :] = jnp.broadcast_to(columns[16 * i : 16 * i + 16, 2:3], (16, 128))
        both = loc[chunk(c), :]
        scale_d = weight * jnp.exp(both[:, 0:1] - columns[:, 0:1])
        scale_t = weight * jnp.exp(both[:, 2:3] - columns[:, 1:2])
        mine = rows(c, y)
        grad[mine, 0:vocab] = (ed[chunk(c), :] * scale_d - et[chunk(c), :] * scale_t).astype(BF16)
        grad[mine, vocab:padded] = jnp.zeros((SIZE[c], padded - vocab), BF16)
        block = grad.at[mine]
        send(f"gp{c}", block, block, at(yy=yp))
        send(f"gm{c}", block, block, at(yy=ym))
        send(f"gs{c}", block, block, sibling)

    def stage_f(c):
        low, high = halves
        arrived(f"gp{c}")
        part_of = grad.at[rows(c, ym), low]
        send(f"fp{c}", part_of, part_of, at(yy=yp))
        block = grad.at[rows(c, ym)]
        send(f"fsm{c}", block, block, sibling)
        arrived(f"gm{c}")
        part_of = grad.at[rows(c, yp), high]
        send(f"fm{c}", part_of, part_of, at(yy=ym))
        block = grad.at[rows(c, yp)]
        send(f"fsp{c}", block, block, sibling)

    def stage_h(c):
        arrived(f"fp{c}")
        arrived(f"fm{c}")
        block = grad.at[rows(c, yo)]
        send(f"hs{c}", block, block, sibling)

    def hrows(c, xx, k, count=1):
        return span(8 * BASE[c] + xx * 2 * SIZE[c] + k * SIZE[c], count * SIZE[c])

    def stage_k(c):
        for name in ("gs", "fsm", "fsp", "hs"):
            arrived(f"{name}{c}")
        out = jnp.dot(
            grad[pl.ds(8 * BASE[c], 8 * SIZE[c]), 0:vocab], head_s[...], preferred_element_type=F32
        )
        for k in (0, 1):
            for xx in range(4):
                start = (k * 4 + xx) * SIZE[c]
                hgp[hrows(c, xx, k), :] = out[start : start + SIZE[c]]
        both = (pl.ds(2 * BASE[c], SIZE[c]), pl.ds(2 * BASE[c] + SIZE[c], SIZE[c]))
        send(f"xap{c}", hgp.at[hrows(c, xo, 0)], xa_r.at[0, chunk(c)], at(xx=xp))
        send(f"xam{c}", hgp.at[hrows(c, xo, 1)], xa_r.at[1, chunk(c)], at(xx=xm))
        send(f"xdp{c}", hgp.at[hrows(c, xp, 1)], xb_r.at[0, both[1]], at(xx=xp))
        send(f"xdm{c}", hgp.at[hrows(c, xm, 0)], xb_r.at[1, both[0]], at(xx=xm))

    def stage_r(c):
        both = (pl.ds(2 * BASE[c], SIZE[c]), pl.ds(2 * BASE[c] + SIZE[c], SIZE[c]))
        arrived(f"xap{c}")
        mine = hrows(c, xp, 0)
        hgp[mine, :] = hgp[mine, :] + xa_r[0, chunk(c)]
        send(f"xbp{c}", hgp.at[mine], xb_r.at[0, both[0]], at(xx=xp))
        arrived(f"xam{c}")
        mine = hrows(c, xm, 1)
        hgp[mine, :] = hgp[mine, :] + xa_r[1, chunk(c)]
        send(f"xbm{c}", hgp.at[mine], xb_r.at[1, both[1]], at(xx=xm))

    def zrows(c, k, i):
        return span(8 * BASE[c] + x * 2 * SIZE[c] + k * SIZE[c] + i * 16, 16)

    def stage_z(c):
        for name in ("xdp", "xdm", "xbp", "xbm"):
            arrived(f"{name}{c}")
        mine = hrows(c, x, 0, 2)
        both = pl.ds(2 * BASE[c], 2 * SIZE[c])
        hgp[mine, :] = hgp[mine, :] + xb_r[0, both] + xb_r[1, both]
        for d_ in range(1, 8):
            zz = (z + d_) % 8
            for i, g in enumerate(CHUNKS[c]):
                copy = remote(f"z{d_}{i}{c}", hgp.at[zrows(c, zz // 4, i)], zr.at[c, d_ - 1], at(zz=zz))
                pl.when(zz % 4 == g // 2)(copy.start)

    def stage_o(c):
        for i, g in enumerate(CHUNKS[c]):

            @pl.when(z % 4 == g // 2)
            def _():
                total = hgp[zrows(c, z // 4, i), :]
                for d_ in range(1, 8):
                    arrived(f"z{d_}{i}{c}")
                    total = total + zr[c, d_ - 1]
                hgrad[pl.ds(16 * (g % 2), 16), :] = total.astype(BF16)

    def stage_w(quarter):
        for cols in tiles(WIDE)[2 * quarter : 2 * quarter + 2]:
            total = None
            for c in range(N):
                term = lax.dot_general(
                    grad[pl.ds(8 * BASE[c], 8 * SIZE[c]), cols], hidden_rows(c),
                    (((0,), (0,)), ((), ())), preferred_element_type=F32,
                )
                total = term if total is None else total + term
            wgrad[cols, :] = total.astype(BF16)

    stages = {
        "M": stage_m, "A": stage_a, "B": stage_b, "L": stage_l, "X": stage_x, "G": stage_g, "F": stage_f,
        "H": stage_h, "K": stage_k, "R": stage_r, "Z": stage_z, "O": stage_o, "W": stage_w, "T": stage_t,
    }
    for entry in ORDER:
        stages[entry[0]](int(entry[1]))

    div[...] = divcol[...].T[0:1, :]
    for name, copy in copies.items():
        if name[0] == "z":
            d_, i, c = (int(v) for v in name[1:])
            pl.when((z + d_) % 4 == CHUNKS[c][i] // 2)(copy.wait_send)
        else:
            copy.wait_send()


def per_device(hidden, target, head, cotangent):
    depth, vocab = head.shape
    padded = -(-vocab // 256) * 256
    vmem = pltpu.VMEM
    results = (
        jax.ShapeDtypeStruct((vocab, depth), BF16),
        jax.ShapeDtypeStruct((32, depth), BF16),
        jax.ShapeDtypeStruct((1, 128), F32),
    )
    wgrad, hgrad, div = pl.pallas_call(
        kernel,
        out_shape=tuple(vmem(r.shape, r.dtype) for r in results),
        in_specs=[pl.BlockSpec(memory_space=pltpu.HBM)] * 4,
        out_specs=(pl.BlockSpec(memory_space=vmem),) * 3,
        scratch_shapes=[
            vmem((vocab, 128), BF16),
            vmem((128, vocab), F32),
            vmem((vocab, depth), BF16),
            vmem((1024, padded), F32),
            vmem((512, padded), F32),
            vmem((2, 128, padded // 2), F32),
            vmem((2, 128, padded), F32),
            vmem((128, vocab), F32),
            vmem((128, vocab), F32),
            vmem((128, 128), F32),
            vmem((128, 128), F32),
            vmem((N, 4, 8, 128), F32),
            vmem((N, 8, 8, 128), F32),
            vmem((128, 128), F32),
            vmem((128, 128), F32),
            vmem((1024, padded), BF16),
            vmem((1024, depth), F32),
            vmem((2, 128, depth), F32),
            vmem((2, 256, depth), F32),
            vmem((N, 7, 16, depth), F32),
            pltpu.SemaphoreType.DMA((48,)),
            pltpu.SemaphoreType.DMA((46 * N,)),
            pltpu.SemaphoreType.DMA((46 * N,)),
        ]
        + [vmem((2, 4, len(groups), 16, depth), BF16) for groups in CHUNKS],
        compiler_params=pltpu.CompilerParams(
            collective_id=0, has_side_effects=True, vmem_limit_bytes=52 * 1024 * 1024
        ),
    )(
        *(
            pltpu.with_memory_space_constraint(v, pltpu.HBM)
            for v in (hidden.reshape(4, 2, 8, 16, depth), target.T, head.T, cotangent.reshape(8, 128))
        )
    )
    wgrad, hgrad, div = pl.pallas_call(
        place,
        out_shape=results,
        in_specs=[pl.BlockSpec(memory_space=vmem)] * 3,
        out_specs=(pl.BlockSpec(memory_space=pltpu.HBM),) * 3,
        scratch_shapes=[pltpu.SemaphoreType.DMA((16,))],
        compiler_params=pltpu.CompilerParams(vmem_limit_bytes=1024 * 1024),
    )(*(pltpu.with_memory_space_constraint(v, vmem) for v in (wgrad, hgrad, div)))
    return hgrad, wgrad.T, div.reshape(128)


def solution(mesh):
    return jax.shard_map(
        per_device,
        mesh=mesh,
        in_specs=(P(None, "hid"), P(None, "voc"), P("hid", "voc"), P()),
        out_specs=(P("voc", "hid"), P("hid", "voc"), P("hid")),
        check_vma=False,
    )
```

```python
import jax
import jax.numpy as jnp
from jax import lax
from jax.experimental import pallas as pl
from jax.experimental.pallas import tpu as pltpu
from jax.sharding import PartitionSpec as P

MESH = pl.DeviceIdType.MESH
F32, BF16 = jnp.float32, jnp.bfloat16
CHUNKS = ((0,), (2, 4), (6, 1), (3, 5), (7,))
N = len(CHUNKS)
SIZE = [16 * len(groups) for groups in CHUNKS]
BASE = [sum(SIZE[:c]) for c in range(N)]
WIDE = 256
EARLY = 3
ORDER = (
    "M0", "M1", "A0", "A1", "T0", "B0", "M2", "B1", "A2", "L0", "M3", "X0", "L1", "B2", "M4", "G0", "A3", "X1",
    "L2", "F0", "G1", "X2", "H0", "B3", "K0", "F1", "G2", "L3", "R0", "H1", "A4", "X3", "K1", "F2", "B4", "G3",
    "R1", "Z0", "H2", "L4", "K2", "X4", "F3", "Z1", "V2", "V0", "H3", "R2", "G4", "K3", "Z2", "F4", "R3", "V1",
    "H4", "K4", "Z3", "R4", "W1", "Z4", "O2", "W2", "O1", "V3", "W0", "W3", "O3", "O0", "O4",
)


def pack(value):
    width = value.shape[1]
    half = -(-width // 256) * 128
    top = value.astype(BF16)
    near = top.astype(F32)
    rest = (value - near) * (256.0 * 127.0) * pltpu.reciprocal(jnp.maximum(jnp.abs(near), 1e-30), approx=True)
    first, second = rest[:, :half], rest[:, half:] * (63.0 / 127.0)
    if width < 2 * half:
        second = jnp.concatenate([second, jnp.zeros((value.shape[0], 2 * half - width), F32)], axis=1)
    first = jnp.round(jnp.clip(first, -127.0, 127.0))
    second = jnp.round(jnp.clip(second, -63.0, 63.0))
    size = 128.0 + jnp.abs(first)
    word = jnp.where(first < 0, -size, size) * jnp.exp2(second)
    return jnp.concatenate([top, word.astype(BF16)], axis=1)


def unpack(packed, width):
    half = -(-width // 256) * 128
    near = packed[:, :width].astype(F32)
    word = packed[:, width:].astype(F32)
    size = jnp.abs(word)
    second = jnp.floor(jnp.log2(size) + 0.001) - 7.0
    first = jnp.round(size * jnp.exp2(-second)) - 128.0
    first = jnp.where(word < 0, -first, first)
    rest = jnp.concatenate([first * (1 / 127.0), second[:, : width - half] * (1 / 63.0)], axis=1)
    return near + rest * jnp.abs(near) * (1 / 256.0)


def place(*refs):
    sem = refs[-1]
    copies = []
    for src, dst in zip(refs[:3], refs[3:6]):
        step = -(-src.shape[0] // 64) * 16
        for i in range(0, src.shape[0], step):
            span = pl.ds(i, min(step, src.shape[0] - i))
            copies.append(pltpu.make_async_copy(src.at[span], dst.at[span], sem.at[len(copies)]))
    for copy in copies:
        copy.start()
    for copy in copies:
        copy.wait()


def kernel(
    hidden, target, head, cot, wgrad, hgrad, div,
    tgt_in, tgt_s, head_s, part, sib_r, ys, ya_r, yb_r, ed, et, loc, turn, stx, stz, cotcol, divcol,
    early, grad, hgp, xs, xa_r, xb_r, zs, zr, load_sem, send_sem, recv_sem, *hid_s,
):
    hid, voc = lax.axis_index("hid"), lax.axis_index("voc")
    y, core = hid // 2, hid % 2
    x, z = voc // 8, voc % 8
    vocab, depth = head.shape
    padded = part.shape[1]
    halves = (pl.ds(0, padded // 2), pl.ds(padded // 2, padded // 2))

    def at(yy=y, cc=core, xx=x, zz=z):
        return {"hid": yy * 2 + cc, "voc": xx * 8 + zz}

    yp, ym, yo = (y + 1) % 4, (y + 3) % 4, (y + 2) % 4
    xp, xm, xo = (x + 1) % 4, (x + 3) % 4, (x + 2) % 4
    sibling = at(cc=1 - core)
    partners = [sibling, at(yy=yp), at(yy=ym)]
    partners += [at(xx=(x + d) % 4) for d in (1, 2, 3)]
    partners += [at(zz=(z + d) % 8) for d in range(1, 8)]

    barrier = pltpu.get_barrier_semaphore()
    for partner in partners:
        pl.semaphore_signal(barrier, inc=1, device_id=partner, device_id_type=MESH)

    loads = {}

    def load(name, src, dst):
        copy = pltpu.make_async_copy(src, dst, load_sem.at[sum(map(len, loads.values()))])
        copy.start()
        loads.setdefault(name, []).append(copy)

    def load_hidden(c):
        for i, g in enumerate(CHUNKS[c]):
            for k in (0, 1):
                load(c, hidden.at[:, k, g], hid_s[c].at[k, :, i])

    def loaded(name):
        for copy in loads[name]:
            copy.wait()

    load_hidden(0)
    for i in range(0, vocab, 512):
        span = pl.ds(i, min(512, vocab - i))
        load("head", head.at[span], head_s.at[span])
    load("target", target.at[:, pl.ds(pl.multiple_of(hid * 128, 128), 128)], tgt_in)
    load("cot", cot, cotcol.at[pl.ds(0, 8)])
    for c in range(1, N):
        load_hidden(c)

    copies = {}

    def remote(name, src, dst, device):
        n = len(copies)
        copy = pltpu.make_async_remote_copy(
            src_ref=src, dst_ref=dst, send_sem=send_sem.at[n], recv_sem=recv_sem.at[n],
            device_id=device, device_id_type=MESH,
        )
        copies[name] = copy
        return copy

    def send(name, src, dst, device):
        remote(name, src, dst, device).start()

    def arrived(name):
        copies[name].wait_recv()

    def span(base, count):
        return pl.ds(base if isinstance(base, int) else pl.multiple_of(base, 16), count)

    def rows(c, yy, cc=core):
        return span(8 * BASE[c] + cc * 4 * SIZE[c] + yy * SIZE[c], SIZE[c])

    def chunk(c):
        return pl.ds(BASE[c], SIZE[c])

    def tiles(width):
        return [pl.ds(i, min(width, vocab - i)) for i in range(0, vocab, width)]

    def hidden_rows(c):
        return hid_s[c][...].reshape(8 * SIZE[c], depth)

    def stage_m(c):
        loaded(c)
        if c == 0:
            loaded("head")
        mine = pl.ds(8 * BASE[c], 8 * SIZE[c])
        for cols in tiles(512):
            part[mine, cols] = lax.dot_general(
                hidden_rows(c), head_s[cols, :], (((1,), (1,)), ((), ())), preferred_element_type=F32
            )
        part[mine, vocab:padded] = jnp.zeros((8 * SIZE[c], padded - vocab), F32)
        if c == 0:
            pl.semaphore_wait(barrier, len(partners))
        theirs = span(8 * BASE[c] + (1 - core) * 4 * SIZE[c], 4 * SIZE[c])
        send(f"sib{c}", part.at[theirs], sib_r.at[pl.ds(4 * BASE[c], 4 * SIZE[c])], sibling)

    def partial(c, yy, half):
        return part[rows(c, yy), half] + sib_r[span(4 * BASE[c] + yy * SIZE[c], SIZE[c]), half]

    def send_packed(name, c, buffer, value, dst, device):
        buffer[chunk(c), :] = pack(value)
        send(f"{name}{c}", buffer.at[chunk(c)], dst, device)

    def stage_a(c):
        low, high = halves
        arrived(f"sib{c}")
        send_packed("yap", c, ys.at[0], partial(c, yo, low), ya_r.at[0, chunk(c)], at(yy=yp))
        send_packed("yam", c, ys.at[1], partial(c, yo, high), ya_r.at[1, chunk(c)], at(yy=ym))
        send_packed("ydp", c, ys.at[2], partial(c, yp, high), yb_r.at[0, 1, chunk(c)], at(yy=yp))
        send_packed("ydm", c, ys.at[3], partial(c, ym, low), yb_r.at[1, 0, chunk(c)], at(yy=ym))

    def stage_b(c):
        low, high = halves
        arrived(f"yap{c}")
        total = partial(c, yp, low) + unpack(ya_r[0, chunk(c)], padded // 2)
        send_packed("ybp", c, ys.at[4], total, yb_r.at[0, 0, chunk(c)], at(yy=yp))
        arrived(f"yam{c}")
        total = partial(c, ym, high) + unpack(ya_r[1, chunk(c)], padded // 2)
        send_packed("ybm", c, ys.at[5], total, yb_r.at[1, 1, chunk(c)], at(yy=ym))

    def own_rows(c):
        return [pl.ds(16 * g, 16) for g in CHUNKS[c]]

    def stage_t(_):
        turn[...] = jnp.zeros_like(turn)
        loaded("cot")
        cotcol[...] = jnp.broadcast_to(cotcol[pl.ds(hid, 1), :], (128, 128)).T
        loaded("target")
        tgt_s[...] = tgt_in[...].astype(F32).T

    def stage_l(c):
        for name in ("ydp", "ydm", "ybp", "ybm"):
            arrived(f"{name}{c}")
        d = [
            partial(c, y, half)
            + unpack(yb_r[0, i, chunk(c)], padded // 2)
            + unpack(yb_r[1, i, chunk(c)], padded // 2)
            for i, half in enumerate(halves)
        ]
        d = jnp.concatenate([d[0], d[1][:, : vocab - padded // 2]], axis=1)
        t = jnp.concatenate([tgt_s[r, :] for r in own_rows(c)], axis=0)
        top_d = jnp.max(d, axis=1, keepdims=True)
        top_t = jnp.max(t, axis=1, keepdims=True)
        exp_d = jnp.exp(d - top_d)
        exp_t = jnp.exp(t - top_t)
        ed[chunk(c), :] = exp_d
        et[chunk(c), :] = exp_t
        sum_d = jnp.sum(exp_d, axis=1, keepdims=True)
        sum_t = jnp.sum(exp_t, axis=1, keepdims=True)
        numer = jnp.sum(exp_t * (t - d), axis=1, keepdims=True)
        lane = lax.broadcasted_iota(jnp.int32, (SIZE[c], 128), 1)
        both = jnp.zeros((SIZE[c], 128), F32)
        for k, column in enumerate((top_d, sum_d, top_t, sum_t, numer)):
            both = jnp.where(lane == k, column, both)
        loc[chunk(c), :] = both
        turn[pl.ds(0, SIZE[c]), :] = both
        stx[c, x] = turn[...].T[0:8, :]
        for d_ in (1, 2, 3):
            send(f"sx{d_}_{c}", stx.at[c, x], stx.at[c, x], at(xx=(x + d_) % 4))

    def merge(stats):
        top_d, top_t = stats[0][0:1], stats[0][2:3]
        for s in stats[1:]:
            top_d, top_t = jnp.maximum(top_d, s[0:1]), jnp.maximum(top_t, s[2:3])
        sum_d = sum_t = numer = jnp.zeros((1, 128), F32)
        for s in stats:
            scale_d, scale_t = jnp.exp(s[0:1] - top_d), jnp.exp(s[2:3] - top_t)
            sum_d, sum_t = sum_d + s[1:2] * scale_d, sum_t + s[3:4] * scale_t
            numer = numer + s[4:5] * scale_t
        return top_d, sum_d, top_t, sum_t, numer

    def stack(values):
        sub = lax.broadcasted_iota(jnp.int32, (8, 128), 0)
        both = jnp.zeros((8, 128), F32)
        for k, row in enumerate(values):
            both = jnp.where(sub == k, row, both)
        return both

    def stage_x(c):
        for d_ in (1, 2, 3):
            arrived(f"sx{d_}_{c}")
        stz[c, z] = stack(merge([stx[c, i] for i in range(4)]))
        for d_ in range(1, 8):
            send(f"sz{d_}_{c}", stz.at[c, z], stz.at[c, z], at(zz=(z + d_) % 8))

    def stage_g(c):
        for d_ in range(1, 8):
            arrived(f"sz{d_}_{c}")
        top_d, sum_d, top_t, sum_t, numer = merge([stz[c, i] for i in range(8)])
        norm_d, norm_t = top_d + jnp.log(sum_d), top_t + jnp.log(sum_t)
        divergence = numer / sum_t + norm_d - norm_t
        turn[pl.ds(0, 8), :] = stack((norm_d, norm_t, divergence))
        columns = turn[...].T[0 : SIZE[c], :]
        weight = jnp.concatenate([cotcol[r, :] for r in own_rows(c)], axis=0)[:, 0:1]
        for i, r in enumerate(own_rows(c)):
            divcol[r, :] = jnp.broadcast_to(columns[16 * i : 16 * i + 16, 2:3], (16, 128))
        both = loc[chunk(c), :]
        scale_d = weight * jnp.exp(both[:, 0:1] - columns[:, 0:1])
        scale_t = weight * jnp.exp(both[:, 2:3] - columns[:, 1:2])
        mine = rows(c, y)
        grad[mine, 0:vocab] = (ed[chunk(c), :] * scale_d - et[chunk(c), :] * scale_t).astype(BF16)
        grad[mine, vocab:padded] = jnp.zeros((SIZE[c], padded - vocab), BF16)
        block = grad.at[mine]
        send(f"gp{c}", block, block, at(yy=yp))
        send(f"gm{c}", block, block, at(yy=ym))
        send(f"gs{c}", block, block, sibling)

    def stage_f(c):
        low, high = halves
        arrived(f"gp{c}")
        part_of = grad.at[rows(c, ym), low]
        send(f"fp{c}", part_of, part_of, at(yy=yp))
        block = grad.at[rows(c, ym)]
        send(f"fsm{c}", block, block, sibling)
        arrived(f"gm{c}")
        part_of = grad.at[rows(c, yp), high]
        send(f"fm{c}", part_of, part_of, at(yy=ym))
        block = grad.at[rows(c, yp)]
        send(f"fsp{c}", block, block, sibling)

    def stage_h(c):
        arrived(f"fp{c}")
        arrived(f"fm{c}")
        block = grad.at[rows(c, yo)]
        send(f"hs{c}", block, block, sibling)

    def hrows(c, xx, k, count=1):
        return span(8 * BASE[c] + xx * 2 * SIZE[c] + k * SIZE[c], count * SIZE[c])

    def stage_k(c):
        for name in ("gs", "fsm", "fsp", "hs"):
            arrived(f"{name}{c}")
        out = jnp.dot(
            grad[pl.ds(8 * BASE[c], 8 * SIZE[c]), 0:vocab], head_s[...], preferred_element_type=F32
        )
        for k in (0, 1):
            for xx in range(4):
                start = (k * 4 + xx) * SIZE[c]
                hgp[hrows(c, xx, k), :] = out[start : start + SIZE[c]]
        send_packed("xap", c, xs.at[0], hgp[hrows(c, xo, 0), :], xa_r.at[0, chunk(c)], at(xx=xp))
        send_packed("xam", c, xs.at[1], hgp[hrows(c, xo, 1), :], xa_r.at[1, chunk(c)], at(xx=xm))
        send_packed("xdp", c, xs.at[2], hgp[hrows(c, xp, 1), :], xb_r.at[0, 1, chunk(c)], at(xx=xp))
        send_packed("xdm", c, xs.at[3], hgp[hrows(c, xm, 0), :], xb_r.at[1, 0, chunk(c)], at(xx=xm))

    def stage_r(c):
        arrived(f"xap{c}")
        total = hgp[hrows(c, xp, 0), :] + unpack(xa_r[0, chunk(c)], depth)
        send_packed("xbp", c, xs.at[4], total, xb_r.at[0, 0, chunk(c)], at(xx=xp))
        arrived(f"xam{c}")
        total = hgp[hrows(c, xm, 1), :] + unpack(xa_r[1, chunk(c)], depth)
        send_packed("xbm", c, xs.at[5], total, xb_r.at[1, 1, chunk(c)], at(xx=xm))

    def zrows(c, k, i):
        return span(8 * BASE[c] + x * 2 * SIZE[c] + k * SIZE[c] + i * 16, 16)

    def stage_z(c):
        for name in ("xdp", "xdm", "xbp", "xbm"):
            arrived(f"{name}{c}")
        for k in (0, 1):
            total = hgp[hrows(c, x, k), :]
            total = total + unpack(xb_r[0, k, chunk(c)], depth) + unpack(xb_r[1, k, chunk(c)], depth)
            hgp[hrows(c, x, k), :] = total
            zs[k, chunk(c), :] = pack(total)
        for d_ in range(1, 8):
            zz = (z + d_) % 8
            for i, g in enumerate(CHUNKS[c]):
                block = zs.at[zz // 4, pl.ds(BASE[c] + 16 * i, 16)]
                copy = remote(f"z{d_}{i}{c}", block, zr.at[c, d_ - 1], at(zz=zz))
                pl.when(zz % 4 == g // 2)(copy.start)

    def stage_o(c):
        for i, g in enumerate(CHUNKS[c]):

            @pl.when(z % 4 == g // 2)
            def _():
                total = hgp[zrows(c, z // 4, i), :]
                for d_ in range(1, 8):
                    arrived(f"z{d_}{i}{c}")
                    total = total + unpack(zr[c, d_ - 1], depth)
                hgrad[pl.ds(16 * (g % 2), 16), :] = total.astype(BF16)

    def head_term(cols, chunks):
        total = None
        for c in chunks:
            term = lax.dot_general(
                grad[pl.ds(8 * BASE[c], 8 * SIZE[c]), cols], hidden_rows(c),
                (((0,), (0,)), ((), ())), preferred_element_type=F32,
            )
            total = term if total is None else total + term
        return total

    def stage_v(quarter):
        for cols in tiles(WIDE)[2 * quarter : 2 * quarter + 2]:
            early[cols, :] = head_term(cols, range(EARLY))

    def stage_w(quarter):
        for cols in tiles(WIDE)[2 * quarter : 2 * quarter + 2]:
            wgrad[cols, :] = (early[cols, :] + head_term(cols, range(EARLY, N))).astype(BF16)

    stages = {
        "M": stage_m, "A": stage_a, "B": stage_b, "L": stage_l, "X": stage_x, "G": stage_g, "F": stage_f,
        "H": stage_h, "K": stage_k, "R": stage_r, "Z": stage_z, "O": stage_o, "V": stage_v, "W": stage_w, "T": stage_t,
    }
    for entry in ORDER:
        stages[entry[0]](int(entry[1]))

    div[...] = divcol[...].T[0:1, :]
    for name, copy in copies.items():
        if name[0] == "z":
            d_, i, c = (int(v) for v in name[1:])
            pl.when((z + d_) % 4 == CHUNKS[c][i] // 2)(copy.wait_send)
        else:
            copy.wait_send()


def per_device(hidden, target, head, cotangent):
    depth, vocab = head.shape
    padded = -(-vocab // 256) * 256
    wide = depth + -(-depth // 256) * 128
    vmem = pltpu.VMEM
    results = (
        jax.ShapeDtypeStruct((vocab, depth), BF16),
        jax.ShapeDtypeStruct((32, depth), BF16),
        jax.ShapeDtypeStruct((1, 128), F32),
    )
    wgrad, hgrad, div = pl.pallas_call(
        kernel,
        out_shape=tuple(vmem(r.shape, r.dtype) for r in results),
        in_specs=[pl.BlockSpec(memory_space=pltpu.HBM)] * 4,
        out_specs=(pl.BlockSpec(memory_space=vmem),) * 3,
        scratch_shapes=[
            vmem((vocab, 128), BF16),
            vmem((128, vocab), F32),
            vmem((vocab, depth), BF16),
            vmem((1024, padded), F32),
            vmem((512, padded), F32),
            vmem((6, 128, padded * 3 // 4), BF16),
            vmem((2, 128, padded * 3 // 4), BF16),
            vmem((2, 2, 128, padded * 3 // 4), BF16),
            vmem((128, vocab), F32),
            vmem((128, vocab), F32),
            vmem((128, 128), F32),
            vmem((128, 128), F32),
            vmem((N, 4, 8, 128), F32),
            vmem((N, 8, 8, 128), F32),
            vmem((128, 128), F32),
            vmem((128, 128), F32),
            vmem((vocab, depth), F32),
            vmem((1024, padded), BF16),
            vmem((1024, depth), F32),
            vmem((6, 128, wide), BF16),
            vmem((2, 128, wide), BF16),
            vmem((2, 2, 128, wide), BF16),
            vmem((2, 128, wide), BF16),
            vmem((N, 7, 16, wide), BF16),
            pltpu.SemaphoreType.DMA((48,)),
            pltpu.SemaphoreType.DMA((46 * N,)),
            pltpu.SemaphoreType.DMA((46 * N,)),
        ]
        + [vmem((2, 4, len(groups), 16, depth), BF16) for groups in CHUNKS],
        compiler_params=pltpu.CompilerParams(
            collective_id=0, has_side_effects=True, vmem_limit_bytes=54 * 1024 * 1024
        ),
    )(
        *(
            pltpu.with_memory_space_constraint(v, pltpu.HBM)
            for v in (hidden.reshape(4, 2, 8, 16, depth), target.T, head.T, cotangent.reshape(8, 128))
        )
    )
    wgrad, hgrad, div = pl.pallas_call(
        place,
        out_shape=results,
        in_specs=[pl.BlockSpec(memory_space=vmem)] * 3,
        out_specs=(pl.BlockSpec(memory_space=pltpu.HBM),) * 3,
        scratch_shapes=[pltpu.SemaphoreType.DMA((16,))],
        compiler_params=pltpu.CompilerParams(vmem_limit_bytes=1024 * 1024),
    )(*(pltpu.with_memory_space_constraint(v, vmem) for v in (wgrad, hgrad, div)))
    return hgrad, wgrad.T, div.reshape(128)


def solution(mesh):
    return jax.shard_map(
        per_device,
        mesh=mesh,
        in_specs=(P(None, "hid"), P(None, "voc"), P("hid", "voc"), P()),
        out_specs=(P("voc", "hid"), P("hid", "voc"), P("hid")),
        check_vma=False,
    )
```

```python
import jax
import jax.numpy as jnp
from jax import lax
from jax.experimental import pallas as pl
from jax.experimental.pallas import tpu as pltpu
from jax.sharding import PartitionSpec as P

MESH = pl.DeviceIdType.MESH
F32, BF16 = jnp.float32, jnp.bfloat16
CHUNKS = ((0,), (4,), (2, 6), (1, 5), (3,), (7,))
N = len(CHUNKS)
SIZE = [16 * len(groups) for groups in CHUNKS]
BASE = [sum(SIZE[:c]) for c in range(N)]
WIDE = 256
EARLY = 4
ORDER = (
    "M0", "M1", "A0", "M2", "A1", "M3", "B0", "A2", "M4", "T0", "B1", "A3", "B2", "M5", "L0", "L1", "A5", "X0",
    "X1", "G0", "B5", "L2", "G1", "B3", "X2", "L5", "F0", "A4", "F1", "X5", "L3", "H0", "G2", "X3", "B4", "K0",
    "H1", "G5", "K1", "R0", "F2", "G3", "L4", "X4", "H2", "R1", "F5", "K2", "F3", "Z0", "H5", "G4", "Z1", "K5",
    "H3", "R2", "K3", "F4", "V2", "Z2", "R5", "H4", "R3", "K4", "Z5", "Z3", "O1", "R4", "V0", "O2", "W2", "Z4",
    "O5", "V3", "V1", "W0", "O0", "W1", "W3", "O3", "O4",
)


def pack(value):
    half = value.shape[1] // 2
    top = value.astype(BF16)
    near = top.astype(F32)
    rest = (value - near) * (256.0 * 127.0) * pltpu.reciprocal(jnp.maximum(jnp.abs(near), 1e-30), approx=True)
    first, second = rest[:, :half], rest[:, half:] * (63.0 / 127.0)
    first = jnp.round(jnp.clip(first, -127.0, 127.0))
    second = jnp.round(jnp.clip(second, -63.0, 63.0))
    size = 128.0 + jnp.abs(first)
    word = jnp.where(first < 0, -size, size) * jnp.exp2(second)
    return jnp.concatenate([top, word.astype(BF16)], axis=1)


def unpack(packed):
    width = packed.shape[1] * 2 // 3
    near = packed[:, :width].astype(F32)
    word = packed[:, width:].astype(F32)
    size = jnp.abs(word)
    second = jnp.floor(jnp.log2(size) + 0.001) - 7.0
    first = jnp.round(size * jnp.exp2(-second)) - 128.0
    first = jnp.where(word < 0, -first, first)
    rest = jnp.concatenate([first * (1 / 127.0), second * (1 / 63.0)], axis=1)
    return near + rest * jnp.abs(near) * (1 / 256.0)


def place(*refs):
    sem = refs[-1]
    copies = []
    for src, dst in zip(refs[:3], refs[3:6]):
        step = -(-src.shape[0] // 64) * 16
        for i in range(0, src.shape[0], step):
            span = pl.ds(i, min(step, src.shape[0] - i))
            copies.append(pltpu.make_async_copy(src.at[span], dst.at[span], sem.at[len(copies)]))
    for copy in copies:
        copy.start()
    for copy in copies:
        copy.wait()


def kernel(
    hidden, target, head, cot, wgrad, hgrad, div,
    tgt_in, tgt_s, head_s, part, sib_r, ys, ya_r, yb_r, ed, et, loc, turn, stx, stz, cotcol, divcol,
    early, grad, hgp, xs, xa_r, xb_r, zs, zr, load_sem, send_sem, recv_sem, *hid_s,
):
    hid, voc = lax.axis_index("hid"), lax.axis_index("voc")
    y, core = hid // 2, hid % 2
    x, z = voc // 8, voc % 8
    vocab, depth = head.shape
    padded = part.shape[1]
    halves = (pl.ds(0, padded // 2), pl.ds(padded // 2, padded // 2))

    def at(yy=y, cc=core, xx=x, zz=z):
        return {"hid": yy * 2 + cc, "voc": xx * 8 + zz}

    yp, ym, yo = (y + 1) % 4, (y + 3) % 4, (y + 2) % 4
    xp, xm, xo = (x + 1) % 4, (x + 3) % 4, (x + 2) % 4
    sibling = at(cc=1 - core)
    partners = [sibling, at(yy=yp), at(yy=ym)]
    partners += [at(xx=(x + d) % 4) for d in (1, 2, 3)]
    partners += [at(zz=(z + d) % 8) for d in range(1, 8)]

    barrier = pltpu.get_barrier_semaphore()
    for partner in partners:
        pl.semaphore_signal(barrier, inc=1, device_id=partner, device_id_type=MESH)

    loads = {}

    def load(name, src, dst):
        copy = pltpu.make_async_copy(src, dst, load_sem.at[sum(map(len, loads.values()))])
        copy.start()
        loads.setdefault(name, []).append(copy)

    def load_hidden(c):
        for i, g in enumerate(CHUNKS[c]):
            for k in (0, 1):
                load(c, hidden.at[:, k, g], hid_s[c].at[k, :, i])

    def loaded(name):
        for copy in loads[name]:
            copy.wait()

    load_hidden(0)
    for i in range(0, vocab, 512):
        rows_of = pl.ds(i, min(512, vocab - i))
        load(f"head{i}", head.at[rows_of], head_s.at[rows_of])
    load_hidden(1)

    def load_rest():
        load("target", target.at[:, pl.ds(pl.multiple_of(hid * 128, 128), 128)], tgt_in)
        load("cot", cot, cotcol.at[pl.ds(0, 8)])
        for c in range(2, N):
            load_hidden(c)

    copies = {}

    def remote(name, src, dst, device):
        n = len(copies)
        copy = pltpu.make_async_remote_copy(
            src_ref=src, dst_ref=dst, send_sem=send_sem.at[n], recv_sem=recv_sem.at[n],
            device_id=device, device_id_type=MESH,
        )
        copies[name] = copy
        return copy

    def send(name, src, dst, device):
        remote(name, src, dst, device).start()

    def arrived(name):
        copies[name].wait_recv()

    def span(base, count):
        return pl.ds(base if isinstance(base, int) else pl.multiple_of(base, 16), count)

    def rows(c, yy, cc=core):
        return span(8 * BASE[c] + cc * 4 * SIZE[c] + yy * SIZE[c], SIZE[c])

    def chunk(c):
        return pl.ds(BASE[c], SIZE[c])

    def tiles(width):
        return [pl.ds(i, min(width, vocab - i)) for i in range(0, vocab, width)]

    def hidden_rows(c):
        return hid_s[c][...].reshape(8 * SIZE[c], depth)

    def stage_m(c):
        loaded(c)
        mine = pl.ds(8 * BASE[c], 8 * SIZE[c])
        for cols in tiles(512):
            if c == 0:
                loaded(f"head{cols.start}")
            part[mine, cols] = lax.dot_general(
                hidden_rows(c), head_s[cols, :], (((1,), (1,)), ((), ())), preferred_element_type=F32
            )
        part[mine, vocab:padded] = jnp.zeros((8 * SIZE[c], padded - vocab), F32)
        if c == 0:
            load_rest()
            pl.semaphore_wait(barrier, len(partners))
        theirs = span(8 * BASE[c] + (1 - core) * 4 * SIZE[c], 4 * SIZE[c])
        send(f"sib{c}", part.at[theirs], sib_r.at[pl.ds(4 * BASE[c], 4 * SIZE[c])], sibling)

    def partial(c, yy, half):
        return part[rows(c, yy), half] + sib_r[span(4 * BASE[c] + yy * SIZE[c], SIZE[c]), half]

    def send_packed(name, c, buffer, value, dst, device):
        buffer[chunk(c), :] = pack(value)
        send(f"{name}{c}", buffer.at[chunk(c)], dst, device)

    def send_rounded(name, c, buffer, value, dst, device):
        buffer[chunk(c), :] = value.astype(BF16)
        send(f"{name}{c}", buffer.at[chunk(c)], dst, device)

    def stage_a(c):
        low, high = halves
        arrived(f"sib{c}")
        send_packed("yap", c, ys.at[0], partial(c, yo, low), ya_r.at[0, chunk(c)], at(yy=yp))
        send_packed("yam", c, ys.at[1], partial(c, yo, high), ya_r.at[1, chunk(c)], at(yy=ym))
        send_packed("ydp", c, ys.at[2], partial(c, yp, high), yb_r.at[0, 1, chunk(c)], at(yy=yp))
        send_packed("ydm", c, ys.at[3], partial(c, ym, low), yb_r.at[1, 0, chunk(c)], at(yy=ym))

    def stage_b(c):
        low, high = halves
        arrived(f"yap{c}")
        total = partial(c, yp, low) + unpack(ya_r[0, chunk(c)])
        send_packed("ybp", c, ys.at[4], total, yb_r.at[0, 0, chunk(c)], at(yy=yp))
        arrived(f"yam{c}")
        total = partial(c, ym, high) + unpack(ya_r[1, chunk(c)])
        send_packed("ybm", c, ys.at[5], total, yb_r.at[1, 1, chunk(c)], at(yy=ym))

    def own_rows(c):
        return [pl.ds(16 * g, 16) for g in CHUNKS[c]]

    def stage_t(_):
        turn[...] = jnp.zeros_like(turn)
        loaded("cot")
        cotcol[...] = jnp.broadcast_to(cotcol[pl.ds(hid, 1), :], (128, 128)).T
        loaded("target")
        tgt_s[...] = tgt_in[...].astype(F32).T

    def stage_l(c):
        for name in ("ydp", "ydm", "ybp", "ybm"):
            arrived(f"{name}{c}")
        d = [
            partial(c, y, half)
            + unpack(yb_r[0, i, chunk(c)])
            + unpack(yb_r[1, i, chunk(c)])
            for i, half in enumerate(halves)
        ]
        d = jnp.concatenate([d[0], d[1][:, : vocab - padded // 2]], axis=1)
        t = jnp.concatenate([tgt_s[r, :] for r in own_rows(c)], axis=0)
        top_d = jnp.max(d, axis=1, keepdims=True)
        top_t = jnp.max(t, axis=1, keepdims=True)
        exp_d = jnp.exp(d - top_d)
        exp_t = jnp.exp(t - top_t)
        ed[chunk(c), :] = exp_d
        et[chunk(c), :] = exp_t
        sum_d = jnp.sum(exp_d, axis=1, keepdims=True)
        sum_t = jnp.sum(exp_t, axis=1, keepdims=True)
        numer = jnp.sum(exp_t * (t - d), axis=1, keepdims=True)
        lane = lax.broadcasted_iota(jnp.int32, (SIZE[c], 128), 1)
        both = jnp.zeros((SIZE[c], 128), F32)
        for k, column in enumerate((top_d, sum_d, top_t, sum_t, numer)):
            both = jnp.where(lane == k, column, both)
        loc[chunk(c), :] = both
        turn[pl.ds(0, SIZE[c]), :] = both
        stx[c, x] = turn[...].T[0:8, :]
        for d_ in (1, 2, 3):
            send(f"sx{d_}_{c}", stx.at[c, x], stx.at[c, x], at(xx=(x + d_) % 4))

    def merge(stats):
        top_d, top_t = stats[0][0:1], stats[0][2:3]
        for s in stats[1:]:
            top_d, top_t = jnp.maximum(top_d, s[0:1]), jnp.maximum(top_t, s[2:3])
        sum_d = sum_t = numer = jnp.zeros((1, 128), F32)
        for s in stats:
            scale_d, scale_t = jnp.exp(s[0:1] - top_d), jnp.exp(s[2:3] - top_t)
            sum_d, sum_t = sum_d + s[1:2] * scale_d, sum_t + s[3:4] * scale_t
            numer = numer + s[4:5] * scale_t
        return top_d, sum_d, top_t, sum_t, numer

    def stack(values):
        sub = lax.broadcasted_iota(jnp.int32, (8, 128), 0)
        both = jnp.zeros((8, 128), F32)
        for k, row in enumerate(values):
            both = jnp.where(sub == k, row, both)
        return both

    def stage_x(c):
        for d_ in (1, 2, 3):
            arrived(f"sx{d_}_{c}")
        stz[c, z] = stack(merge([stx[c, i] for i in range(4)]))
        for d_ in range(1, 8):
            send(f"sz{d_}_{c}", stz.at[c, z], stz.at[c, z], at(zz=(z + d_) % 8))

    def stage_g(c):
        for d_ in range(1, 8):
            arrived(f"sz{d_}_{c}")
        top_d, sum_d, top_t, sum_t, numer = merge([stz[c, i] for i in range(8)])
        norm_d, norm_t = top_d + jnp.log(sum_d), top_t + jnp.log(sum_t)
        divergence = numer / sum_t + norm_d - norm_t
        turn[pl.ds(0, 8), :] = stack((norm_d, norm_t, divergence))
        columns = turn[...].T[0 : SIZE[c], :]
        weight = jnp.concatenate([cotcol[r, :] for r in own_rows(c)], axis=0)[:, 0:1]
        for i, r in enumerate(own_rows(c)):
            divcol[r, :] = jnp.broadcast_to(columns[16 * i : 16 * i + 16, 2:3], (16, 128))
        both = loc[chunk(c), :]
        scale_d = weight * jnp.exp(both[:, 0:1] - columns[:, 0:1])
        scale_t = weight * jnp.exp(both[:, 2:3] - columns[:, 1:2])
        mine = rows(c, y)
        grad[mine, 0:vocab] = (ed[chunk(c), :] * scale_d - et[chunk(c), :] * scale_t).astype(BF16)
        grad[mine, vocab:padded] = jnp.zeros((SIZE[c], padded - vocab), BF16)
        block = grad.at[mine]
        send(f"gp{c}", block, block, at(yy=yp))
        send(f"gm{c}", block, block, at(yy=ym))
        send(f"gs{c}", block, block, sibling)

    def stage_f(c):
        low, high = halves
        arrived(f"gp{c}")
        part_of = grad.at[rows(c, ym), low]
        send(f"fp{c}", part_of, part_of, at(yy=yp))
        block = grad.at[rows(c, ym)]
        send(f"fsm{c}", block, block, sibling)
        arrived(f"gm{c}")
        part_of = grad.at[rows(c, yp), high]
        send(f"fm{c}", part_of, part_of, at(yy=ym))
        block = grad.at[rows(c, yp)]
        send(f"fsp{c}", block, block, sibling)

    def stage_h(c):
        arrived(f"fp{c}")
        arrived(f"fm{c}")
        block = grad.at[rows(c, yo)]
        send(f"hs{c}", block, block, sibling)

    def hrows(c, xx, k, count=1):
        return span(8 * BASE[c] + xx * 2 * SIZE[c] + k * SIZE[c], count * SIZE[c])

    def stage_k(c):
        for name in ("gs", "fsm", "fsp", "hs"):
            arrived(f"{name}{c}")
        out = jnp.dot(
            grad[pl.ds(8 * BASE[c], 8 * SIZE[c]), 0:vocab], head_s[...], preferred_element_type=F32
        )
        for k in (0, 1):
            for xx in range(4):
                start = (k * 4 + xx) * SIZE[c]
                hgp[hrows(c, xx, k), :] = out[start : start + SIZE[c]]
        send_rounded("xap", c, xs.at[0], hgp[hrows(c, xo, 0), :], xa_r.at[0, chunk(c)], at(xx=xp))
        send_rounded("xam", c, xs.at[1], hgp[hrows(c, xo, 1), :], xa_r.at[1, chunk(c)], at(xx=xm))
        send_rounded("xdp", c, xs.at[2], hgp[hrows(c, xp, 1), :], xb_r.at[0, 1, chunk(c)], at(xx=xp))
        send_rounded("xdm", c, xs.at[3], hgp[hrows(c, xm, 0), :], xb_r.at[1, 0, chunk(c)], at(xx=xm))

    def stage_r(c):
        arrived(f"xap{c}")
        total = hgp[hrows(c, xp, 0), :] + xa_r[0, chunk(c)].astype(F32)
        send_rounded("xbp", c, xs.at[4], total, xb_r.at[0, 0, chunk(c)], at(xx=xp))
        arrived(f"xam{c}")
        total = hgp[hrows(c, xm, 1), :] + xa_r[1, chunk(c)].astype(F32)
        send_rounded("xbm", c, xs.at[5], total, xb_r.at[1, 1, chunk(c)], at(xx=xm))

    def zrows(c, k, i):
        return span(8 * BASE[c] + x * 2 * SIZE[c] + k * SIZE[c] + i * 16, 16)

    def stage_z(c):
        for name in ("xdp", "xdm", "xbp", "xbm"):
            arrived(f"{name}{c}")
        for k in (0, 1):
            total = hgp[hrows(c, x, k), :]
            total = total + xb_r[0, k, chunk(c)].astype(F32) + xb_r[1, k, chunk(c)].astype(F32)
            hgp[hrows(c, x, k), :] = total
            zs[k, chunk(c), :] = total.astype(BF16)
        for d_ in range(1, 8):
            zz = (z + d_) % 8
            for i, g in enumerate(CHUNKS[c]):
                block = zs.at[zz // 4, pl.ds(BASE[c] + 16 * i, 16)]
                copy = remote(f"z{d_}{i}{c}", block, zr.at[c, d_ - 1], at(zz=zz))
                pl.when(zz % 4 == g // 2)(copy.start)

    def stage_o(c):
        for i, g in enumerate(CHUNKS[c]):

            @pl.when(z % 4 == g // 2)
            def _():
                total = hgp[zrows(c, z // 4, i), :]
                for d_ in range(1, 8):
                    arrived(f"z{d_}{i}{c}")
                    total = total + zr[c, d_ - 1].astype(F32)
                hgrad[pl.ds(16 * (g % 2), 16), :] = total.astype(BF16)

    def head_term(cols, chunks):
        total = None
        for c in chunks:
            term = lax.dot_general(
                grad[pl.ds(8 * BASE[c], 8 * SIZE[c]), cols], hidden_rows(c),
                (((0,), (0,)), ((), ())), preferred_element_type=F32,
            )
            total = term if total is None else total + term
        return total

    def stage_v(quarter):
        for cols in tiles(WIDE)[2 * quarter : 2 * quarter + 2]:
            early[cols, :] = head_term(cols, range(EARLY))

    def stage_w(quarter):
        for cols in tiles(WIDE)[2 * quarter : 2 * quarter + 2]:
            wgrad[cols, :] = (early[cols, :] + head_term(cols, range(EARLY, N))).astype(BF16)

    stages = {
        "M": stage_m, "A": stage_a, "B": stage_b, "L": stage_l, "X": stage_x, "G": stage_g, "F": stage_f,
        "H": stage_h, "K": stage_k, "R": stage_r, "Z": stage_z, "O": stage_o, "V": stage_v, "W": stage_w, "T": stage_t,
    }
    for entry in ORDER[:-1]:
        stages[entry[0]](int(entry[1]))

    div[...] = divcol[...].T[0:1, :]
    for name, copy in copies.items():
        if name[0] == "z":
            d_, i, c = (int(v) for v in name[1:])
            pl.when((z + d_) % 4 == CHUNKS[c][i] // 2)(copy.wait_send)
        else:
            copy.wait_send()
    stages[ORDER[-1][0]](int(ORDER[-1][1]))


def per_device(hidden, target, head, cotangent):
    depth, vocab = head.shape
    padded = -(-vocab // 256) * 256
    vmem = pltpu.VMEM
    results = (
        jax.ShapeDtypeStruct((vocab, depth), BF16),
        jax.ShapeDtypeStruct((32, depth), BF16),
        jax.ShapeDtypeStruct((1, 128), F32),
    )
    wgrad, hgrad, div = pl.pallas_call(
        kernel,
        out_shape=tuple(vmem(r.shape, r.dtype) for r in results),
        in_specs=[pl.BlockSpec(memory_space=pltpu.HBM)] * 4,
        out_specs=(pl.BlockSpec(memory_space=vmem),) * 3,
        scratch_shapes=[
            vmem((vocab, 128), BF16),
            vmem((128, vocab), F32),
            vmem((vocab, depth), BF16),
            vmem((1024, padded), F32),
            vmem((512, padded), F32),
            vmem((6, 128, padded * 3 // 4), BF16),
            vmem((2, 128, padded * 3 // 4), BF16),
            vmem((2, 2, 128, padded * 3 // 4), BF16),
            vmem((128, vocab), F32),
            vmem((128, vocab), F32),
            vmem((128, 128), F32),
            vmem((128, 128), F32),
            vmem((N, 4, 8, 128), F32),
            vmem((N, 8, 8, 128), F32),
            vmem((128, 128), F32),
            vmem((128, 128), F32),
            vmem((vocab, depth), F32),
            vmem((1024, padded), BF16),
            vmem((1024, depth), F32),
            vmem((6, 128, depth), BF16),
            vmem((2, 128, depth), BF16),
            vmem((2, 2, 128, depth), BF16),
            vmem((2, 128, depth), BF16),
            vmem((N, 7, 16, depth), BF16),
            pltpu.SemaphoreType.DMA((48,)),
            pltpu.SemaphoreType.DMA((46 * N,)),
            pltpu.SemaphoreType.DMA((46 * N,)),
        ]
        + [vmem((2, 4, len(groups), 16, depth), BF16) for groups in CHUNKS],
        compiler_params=pltpu.CompilerParams(
            collective_id=0, has_side_effects=True, vmem_limit_bytes=54 * 1024 * 1024
        ),
    )(
        *(
            pltpu.with_memory_space_constraint(v, pltpu.HBM)
            for v in (hidden.reshape(4, 2, 8, 16, depth), target.T, head.T, cotangent.reshape(8, 128))
        )
    )
    wgrad, hgrad, div = pl.pallas_call(
        place,
        out_shape=results,
        in_specs=[pl.BlockSpec(memory_space=vmem)] * 3,
        out_specs=(pl.BlockSpec(memory_space=pltpu.HBM),) * 3,
        scratch_shapes=[pltpu.SemaphoreType.DMA((16,))],
        compiler_params=pltpu.CompilerParams(vmem_limit_bytes=1024 * 1024),
    )(*(pltpu.with_memory_space_constraint(v, vmem) for v in (wgrad, hgrad, div)))
    return hgrad, wgrad.T, div.reshape(128)


def solution(mesh):
    return jax.shard_map(
        per_device,
        mesh=mesh,
        in_specs=(P(None, "hid"), P(None, "voc"), P("hid", "voc"), P()),
        out_specs=(P("voc", "hid"), P("hid", "voc"), P("hid")),
        check_vma=False,
    )
```

```python
import jax
import jax.numpy as jnp
from jax import lax
from jax.experimental import pallas as pl
from jax.experimental.pallas import tpu as pltpu
from jax.sharding import PartitionSpec as P

MESH = pl.DeviceIdType.MESH
F32, BF16 = jnp.float32, jnp.bfloat16
CHUNKS = ((0,), (4,), (2, 6), (1, 5), (3,), (7,))
N = len(CHUNKS)
SIZE = [16 * len(groups) for groups in CHUNKS]
BASE = [sum(SIZE[:c]) for c in range(N)]
WIDE = 256
EARLY = 4
ORDER = (
    "M0", "M1", "A0", "M2", "A1", "B0", "T0", "A2", "M3", "B1", "L0", "M4", "B2", "M5", "A4", "L1", "A5", "L2",
    "B4", "X1", "X0", "A3", "X2", "L4", "B5", "B3", "G0", "G1", "G2", "X4", "L5", "L3", "X5", "F0", "G4", "X3",
    "F1", "F2", "H0", "G5", "H1", "F4", "G3", "K0", "H2", "K1", "F5", "K2", "H4", "F3", "R0", "H5", "R1", "K4",
    "K5", "R2", "H3", "Z0", "Z1", "R4", "K3", "Z2", "R5", "V2", "Z4", "R3", "V0", "Z5", "O0", "V3", "O1", "W0",
    "Z3", "O4", "V1", "O2", "W3", "W2", "W1", "O5", "O3",
)


def pack(value):
    half = value.shape[1] // 2
    top = value.astype(BF16)
    near = top.astype(F32)
    rest = (value - near) * (256.0 * 127.0) * pltpu.reciprocal(jnp.maximum(jnp.abs(near), 1e-30), approx=True)
    first, second = rest[:, :half], rest[:, half:] * (63.0 / 127.0)
    first = jnp.round(jnp.clip(first, -127.0, 127.0))
    second = jnp.round(jnp.clip(second, -63.0, 63.0))
    size = 128.0 + jnp.abs(first)
    word = jnp.where(first < 0, -size, size) * jnp.exp2(second)
    return jnp.concatenate([top, word.astype(BF16)], axis=1)


def unpack(packed):
    width = packed.shape[1] * 2 // 3
    near = packed[:, :width].astype(F32)
    word = packed[:, width:].astype(F32)
    size = jnp.abs(word)
    second = jnp.floor(jnp.log2(size) + 0.001) - 7.0
    first = jnp.round(size * jnp.exp2(-second)) - 128.0
    first = jnp.where(word < 0, -first, first)
    rest = jnp.concatenate([first * (1 / 127.0), second * (1 / 63.0)], axis=1)
    return near + rest * jnp.abs(near) * (1 / 256.0)


def place(*refs):
    sem = refs[-1]
    copies = []
    for src, dst in zip(refs[:3], refs[3:6]):
        step = -(-src.shape[0] // 64) * 16
        for i in range(0, src.shape[0], step):
            span = pl.ds(i, min(step, src.shape[0] - i))
            copies.append(pltpu.make_async_copy(src.at[span], dst.at[span], sem.at[len(copies)]))
    for copy in copies:
        copy.start()
    for copy in copies:
        copy.wait()


def kernel(
    hidden, target, head, cot, wgrad, hgrad, div,
    tgt_in, tgt_s, head_s, part, sib_r, ys, ya_r, yb_r, ed, et, loc, turn, stx, stz, cotcol, divcol,
    early, grad, hgp, xs, xa_r, xb_r, zs, zr, load_sem, send_sem, recv_sem, *hid_s,
):
    hid, voc = lax.axis_index("hid"), lax.axis_index("voc")
    y, core = hid // 2, hid % 2
    x, z = voc // 8, voc % 8
    vocab, depth = head.shape
    padded = part.shape[1]
    halves = (pl.ds(0, padded // 2), pl.ds(padded // 2, padded // 2))

    def at(yy=y, cc=core, xx=x, zz=z):
        return {"hid": yy * 2 + cc, "voc": xx * 8 + zz}

    yp, ym, yo = (y + 1) % 4, (y + 3) % 4, (y + 2) % 4
    xp, xm, xo = (x + 1) % 4, (x + 3) % 4, (x + 2) % 4
    sibling = at(cc=1 - core)
    partners = [sibling, at(yy=yp), at(yy=ym)]
    partners += [at(xx=(x + d) % 4) for d in (1, 2, 3)]
    partners += [at(zz=(z + d) % 8) for d in range(1, 8)]

    barrier = pltpu.get_barrier_semaphore()
    for partner in partners:
        pl.semaphore_signal(barrier, inc=1, device_id=partner, device_id_type=MESH)

    loads = {}

    def load(name, src, dst):
        copy = pltpu.make_async_copy(src, dst, load_sem.at[sum(map(len, loads.values()))])
        copy.start()
        loads.setdefault(name, []).append(copy)

    def load_hidden(c):
        for i, g in enumerate(CHUNKS[c]):
            for k in (0, 1):
                load(c, hidden.at[:, k, g], hid_s[c].at[k, :, i])

    def loaded(name):
        for copy in loads[name]:
            copy.wait()

    load_hidden(0)
    for i in range(0, vocab, 512):
        rows_of = pl.ds(i, min(512, vocab - i))
        load(f"head{i}", head.at[rows_of], head_s.at[rows_of])
    load_hidden(1)

    def load_rest():
        load("target", target.at[:, pl.ds(pl.multiple_of(hid * 128, 128), 128)], tgt_in)
        load("cot", cot, cotcol.at[pl.ds(0, 8)])
        for c in range(2, N):
            load_hidden(c)

    copies = {}

    def remote(name, src, dst, device):
        n = len(copies)
        copy = pltpu.make_async_remote_copy(
            src_ref=src, dst_ref=dst, send_sem=send_sem.at[n], recv_sem=recv_sem.at[n],
            device_id=device, device_id_type=MESH,
        )
        copies[name] = copy
        return copy

    def send(name, src, dst, device):
        remote(name, src, dst, device).start()

    def arrived(name):
        copies[name].wait_recv()

    def span(base, count):
        return pl.ds(base if isinstance(base, int) else pl.multiple_of(base, 16), count)

    def rows(c, yy, cc=core):
        return span(8 * BASE[c] + cc * 4 * SIZE[c] + yy * SIZE[c], SIZE[c])

    def chunk(c):
        return pl.ds(BASE[c], SIZE[c])

    def tiles(width):
        return [pl.ds(i, min(width, vocab - i)) for i in range(0, vocab, width)]

    def hidden_rows(c):
        return hid_s[c][...].reshape(8 * SIZE[c], depth)

    def stage_m(c):
        loaded(c)
        mine = pl.ds(8 * BASE[c], 8 * SIZE[c])
        for cols in tiles(512):
            if c == 0:
                loaded(f"head{cols.start}")
            part[mine, cols] = lax.dot_general(
                hidden_rows(c), head_s[cols, :], (((1,), (1,)), ((), ())), preferred_element_type=F32
            )
        part[mine, vocab:padded] = jnp.zeros((8 * SIZE[c], padded - vocab), F32)
        if c == 0:
            load_rest()
            pl.semaphore_wait(barrier, len(partners))
        theirs = span(8 * BASE[c] + (1 - core) * 4 * SIZE[c], 4 * SIZE[c])
        send(f"sib{c}", part.at[theirs], sib_r.at[pl.ds(4 * BASE[c], 4 * SIZE[c])], sibling)

    def partial(c, yy, half):
        return part[rows(c, yy), half] + sib_r[span(4 * BASE[c] + yy * SIZE[c], SIZE[c]), half]

    def send_packed(name, c, buffer, value, dst, device):
        buffer[chunk(c), :] = pack(value)
        send(f"{name}{c}", buffer.at[chunk(c)], dst, device)

    def send_rounded(name, c, buffer, value, dst, device):
        buffer[chunk(c), :] = value.astype(BF16)
        send(f"{name}{c}", buffer.at[chunk(c)], dst, device)

    def stage_a(c):
        low, high = halves
        arrived(f"sib{c}")
        send_packed("yap", c, ys.at[0], partial(c, yo, low), ya_r.at[0, chunk(c)], at(yy=yp))
        send_packed("yam", c, ys.at[1], partial(c, yo, high), ya_r.at[1, chunk(c)], at(yy=ym))
        send_packed("ydp", c, ys.at[2], partial(c, yp, high), yb_r.at[0, 1, chunk(c)], at(yy=yp))
        send_packed("ydm", c, ys.at[3], partial(c, ym, low), yb_r.at[1, 0, chunk(c)], at(yy=ym))

    def stage_b(c):
        low, high = halves
        arrived(f"yap{c}")
        total = partial(c, yp, low) + unpack(ya_r[0, chunk(c)])
        send_packed("ybp", c, ys.at[4], total, yb_r.at[0, 0, chunk(c)], at(yy=yp))
        arrived(f"yam{c}")
        total = partial(c, ym, high) + unpack(ya_r[1, chunk(c)])
        send_packed("ybm", c, ys.at[5], total, yb_r.at[1, 1, chunk(c)], at(yy=ym))

    def own_rows(c):
        return [pl.ds(16 * g, 16) for g in CHUNKS[c]]

    def stage_t(_):
        turn[...] = jnp.zeros_like(turn)
        loaded("cot")
        cotcol[...] = jnp.broadcast_to(cotcol[pl.ds(hid, 1), :], (128, 128)).T
        loaded("target")
        tgt_s[...] = tgt_in[...].astype(F32).T

    def stage_l(c):
        for name in ("ydp", "ydm", "ybp", "ybm"):
            arrived(f"{name}{c}")
        d = [
            partial(c, y, half)
            + unpack(yb_r[0, i, chunk(c)])
            + unpack(yb_r[1, i, chunk(c)])
            for i, half in enumerate(halves)
        ]
        d = jnp.concatenate([d[0], d[1][:, : vocab - padded // 2]], axis=1)
        t = jnp.concatenate([tgt_s[r, :] for r in own_rows(c)], axis=0)
        top_d = jnp.max(d, axis=1, keepdims=True)
        top_t = jnp.max(t, axis=1, keepdims=True)
        exp_d = jnp.exp(d - top_d)
        exp_t = jnp.exp(t - top_t)
        ed[chunk(c), :] = exp_d
        et[chunk(c), :] = exp_t
        sum_d = jnp.sum(exp_d, axis=1, keepdims=True)
        sum_t = jnp.sum(exp_t, axis=1, keepdims=True)
        numer = jnp.sum(exp_t * (t - d), axis=1, keepdims=True)
        lane = lax.broadcasted_iota(jnp.int32, (SIZE[c], 128), 1)
        both = jnp.zeros((SIZE[c], 128), F32)
        for k, column in enumerate((top_d, sum_d, top_t, sum_t, numer)):
            both = jnp.where(lane == k, column, both)
        loc[chunk(c), :] = both
        turn[pl.ds(0, SIZE[c]), :] = both
        stx[c, x] = turn[...].T[0:8, :]
        for d_ in (1, 2, 3):
            send(f"sx{d_}_{c}", stx.at[c, x], stx.at[c, x], at(xx=(x + d_) % 4))

    def merge(stats):
        top_d, top_t = stats[0][0:1], stats[0][2:3]
        for s in stats[1:]:
            top_d, top_t = jnp.maximum(top_d, s[0:1]), jnp.maximum(top_t, s[2:3])
        sum_d = sum_t = numer = jnp.zeros((1, 128), F32)
        for s in stats:
            scale_d, scale_t = jnp.exp(s[0:1] - top_d), jnp.exp(s[2:3] - top_t)
            sum_d, sum_t = sum_d + s[1:2] * scale_d, sum_t + s[3:4] * scale_t
            numer = numer + s[4:5] * scale_t
        return top_d, sum_d, top_t, sum_t, numer

    def stack(values):
        sub = lax.broadcasted_iota(jnp.int32, (8, 128), 0)
        both = jnp.zeros((8, 128), F32)
        for k, row in enumerate(values):
            both = jnp.where(sub == k, row, both)
        return both

    def stage_x(c):
        for d_ in (1, 2, 3):
            arrived(f"sx{d_}_{c}")
        stz[c, z] = stack(merge([stx[c, i] for i in range(4)]))
        for d_ in range(1, 8):
            send(f"sz{d_}_{c}", stz.at[c, z], stz.at[c, z], at(zz=(z + d_) % 8))

    def stage_g(c):
        for d_ in range(1, 8):
            arrived(f"sz{d_}_{c}")
        top_d, sum_d, top_t, sum_t, numer = merge([stz[c, i] for i in range(8)])
        norm_d, norm_t = top_d + jnp.log(sum_d), top_t + jnp.log(sum_t)
        divergence = numer / sum_t + norm_d - norm_t
        turn[pl.ds(0, 8), :] = stack((norm_d, norm_t, divergence))
        columns = turn[...].T[0 : SIZE[c], :]
        weight = jnp.concatenate([cotcol[r, :] for r in own_rows(c)], axis=0)[:, 0:1]
        for i, r in enumerate(own_rows(c)):
            divcol[r, :] = jnp.broadcast_to(columns[16 * i : 16 * i + 16, 2:3], (16, 128))
        both = loc[chunk(c), :]
        scale_d = weight * jnp.exp(both[:, 0:1] - columns[:, 0:1])
        scale_t = weight * jnp.exp(both[:, 2:3] - columns[:, 1:2])
        mine = rows(c, y)
        grad[mine, 0:vocab] = (ed[chunk(c), :] * scale_d - et[chunk(c), :] * scale_t).astype(BF16)
        grad[mine, vocab:padded] = jnp.zeros((SIZE[c], padded - vocab), BF16)
        block = grad.at[mine]
        send(f"gp{c}", block, block, at(yy=yp))
        send(f"gm{c}", block, block, at(yy=ym))
        send(f"gs{c}", block, block, sibling)

    def stage_f(c):
        low, high = halves
        arrived(f"gp{c}")
        part_of = grad.at[rows(c, ym), low]
        send(f"fp{c}", part_of, part_of, at(yy=yp))
        block = grad.at[rows(c, ym)]
        send(f"fsm{c}", block, block, sibling)
        arrived(f"gm{c}")
        part_of = grad.at[rows(c, yp), high]
        send(f"fm{c}", part_of, part_of, at(yy=ym))
        block = grad.at[rows(c, yp)]
        send(f"fsp{c}", block, block, sibling)

    def stage_h(c):
        arrived(f"fp{c}")
        arrived(f"fm{c}")
        block = grad.at[rows(c, yo)]
        send(f"hs{c}", block, block, sibling)

    def hrows(c, xx, k, count=1):
        return span(8 * BASE[c] + xx * 2 * SIZE[c] + k * SIZE[c], count * SIZE[c])

    def stage_k(c):
        for name in ("gs", "fsm", "fsp", "hs"):
            arrived(f"{name}{c}")
        out = jnp.dot(
            grad[pl.ds(8 * BASE[c], 8 * SIZE[c]), 0:vocab], head_s[...], preferred_element_type=F32
        )
        for k in (0, 1):
            for xx in range(4):
                start = (k * 4 + xx) * SIZE[c]
                hgp[hrows(c, xx, k), :] = out[start : start + SIZE[c]]
        send_rounded("xap", c, xs.at[0], hgp[hrows(c, xo, 0), :], xa_r.at[0, chunk(c)], at(xx=xp))
        send_rounded("xam", c, xs.at[1], hgp[hrows(c, xo, 1), :], xa_r.at[1, chunk(c)], at(xx=xm))
        send_rounded("xdp", c, xs.at[2], hgp[hrows(c, xp, 1), :], xb_r.at[0, 1, chunk(c)], at(xx=xp))
        send_rounded("xdm", c, xs.at[3], hgp[hrows(c, xm, 0), :], xb_r.at[1, 0, chunk(c)], at(xx=xm))

    def stage_r(c):
        arrived(f"xap{c}")
        total = hgp[hrows(c, xp, 0), :] + xa_r[0, chunk(c)].astype(F32)
        send_rounded("xbp", c, xs.at[4], total, xb_r.at[0, 0, chunk(c)], at(xx=xp))
        arrived(f"xam{c}")
        total = hgp[hrows(c, xm, 1), :] + xa_r[1, chunk(c)].astype(F32)
        send_rounded("xbm", c, xs.at[5], total, xb_r.at[1, 1, chunk(c)], at(xx=xm))

    def zrows(c, k, i):
        return span(8 * BASE[c] + x * 2 * SIZE[c] + k * SIZE[c] + i * 16, 16)

    def stage_z(c):
        for name in ("xdp", "xdm", "xbp", "xbm"):
            arrived(f"{name}{c}")
        for k in (0, 1):
            total = hgp[hrows(c, x, k), :]
            total = total + xb_r[0, k, chunk(c)].astype(F32) + xb_r[1, k, chunk(c)].astype(F32)
            hgp[hrows(c, x, k), :] = total
            zs[k, chunk(c), :] = total.astype(BF16)
        for d_ in range(1, 8):
            zz = (z + d_) % 8
            for i, g in enumerate(CHUNKS[c]):
                block = zs.at[zz // 4, pl.ds(BASE[c] + 16 * i, 16)]
                copy = remote(f"z{d_}{i}{c}", block, zr.at[c, d_ - 1], at(zz=zz))
                pl.when(zz % 4 == g // 2)(copy.start)

    def stage_o(c):
        for i, g in enumerate(CHUNKS[c]):

            @pl.when(z % 4 == g // 2)
            def _():
                total = hgp[zrows(c, z // 4, i), :]
                for d_ in range(1, 8):
                    arrived(f"z{d_}{i}{c}")
                    total = total + zr[c, d_ - 1].astype(F32)
                hgrad[pl.ds(16 * (g % 2), 16), :] = total.astype(BF16)

    def head_term(cols, chunks):
        total = None
        for c in chunks:
            term = lax.dot_general(
                grad[pl.ds(8 * BASE[c], 8 * SIZE[c]), cols], hidden_rows(c),
                (((0,), (0,)), ((), ())), preferred_element_type=F32,
            )
            total = term if total is None else total + term
        return total

    def stage_v(quarter):
        for cols in tiles(WIDE)[2 * quarter : 2 * quarter + 2]:
            early[cols, :] = head_term(cols, range(EARLY))

    def stage_w(quarter):
        for cols in tiles(WIDE)[2 * quarter : 2 * quarter + 2]:
            wgrad[cols, :] = (early[cols, :] + head_term(cols, range(EARLY, N))).astype(BF16)

    stages = {
        "M": stage_m, "A": stage_a, "B": stage_b, "L": stage_l, "X": stage_x, "G": stage_g, "F": stage_f,
        "H": stage_h, "K": stage_k, "R": stage_r, "Z": stage_z, "O": stage_o, "V": stage_v, "W": stage_w, "T": stage_t,
    }
    for entry in ORDER[:-1]:
        stages[entry[0]](int(entry[1]))

    div[...] = divcol[...].T[0:1, :]
    for name, copy in copies.items():
        if name[0] == "z":
            d_, i, c = (int(v) for v in name[1:])
            pl.when((z + d_) % 4 == CHUNKS[c][i] // 2)(copy.wait_send)
        else:
            copy.wait_send()
    stages[ORDER[-1][0]](int(ORDER[-1][1]))


def per_device(hidden, target, head, cotangent):
    depth, vocab = head.shape
    padded = -(-vocab // 256) * 256
    vmem = pltpu.VMEM
    results = (
        jax.ShapeDtypeStruct((vocab, depth), BF16),
        jax.ShapeDtypeStruct((32, depth), BF16),
        jax.ShapeDtypeStruct((1, 128), F32),
    )
    wgrad, hgrad, div = pl.pallas_call(
        kernel,
        out_shape=tuple(vmem(r.shape, r.dtype) for r in results),
        in_specs=[pl.BlockSpec(memory_space=pltpu.HBM)] * 4,
        out_specs=(pl.BlockSpec(memory_space=vmem),) * 3,
        scratch_shapes=[
            vmem((vocab, 128), BF16),
            vmem((128, vocab), F32),
            vmem((vocab, depth), BF16),
            vmem((1024, padded), F32),
            vmem((512, padded), F32),
            vmem((6, 128, padded * 3 // 4), BF16),
            vmem((2, 128, padded * 3 // 4), BF16),
            vmem((2, 2, 128, padded * 3 // 4), BF16),
            vmem((128, vocab), F32),
            vmem((128, vocab), F32),
            vmem((128, 128), F32),
            vmem((128, 128), F32),
            vmem((N, 4, 8, 128), F32),
            vmem((N, 8, 8, 128), F32),
            vmem((128, 128), F32),
            vmem((128, 128), F32),
            vmem((vocab, depth), F32),
            vmem((1024, padded), BF16),
            vmem((1024, depth), F32),
            vmem((6, 128, depth), BF16),
            vmem((2, 128, depth), BF16),
            vmem((2, 2, 128, depth), BF16),
            vmem((2, 128, depth), BF16),
            vmem((N, 7, 16, depth), BF16),
            pltpu.SemaphoreType.DMA((48,)),
            pltpu.SemaphoreType.DMA((46 * N,)),
            pltpu.SemaphoreType.DMA((46 * N,)),
        ]
        + [vmem((2, 4, len(groups), 16, depth), BF16) for groups in CHUNKS],
        compiler_params=pltpu.CompilerParams(
            collective_id=0, has_side_effects=True, vmem_limit_bytes=54 * 1024 * 1024
        ),
    )(
        *(
            pltpu.with_memory_space_constraint(v, pltpu.HBM)
            for v in (hidden.reshape(4, 2, 8, 16, depth), target.T, head.T, cotangent.reshape(8, 128))
        )
    )
    wgrad, hgrad, div = pl.pallas_call(
        place,
        out_shape=results,
        in_specs=[pl.BlockSpec(memory_space=vmem)] * 3,
        out_specs=(pl.BlockSpec(memory_space=pltpu.HBM),) * 3,
        scratch_shapes=[pltpu.SemaphoreType.DMA((16,))],
        compiler_params=pltpu.CompilerParams(vmem_limit_bytes=1024 * 1024),
    )(*(pltpu.with_memory_space_constraint(v, vmem) for v in (wgrad, hgrad, div)))
    return hgrad, wgrad.T, div.reshape(128)


def solution(mesh):
    return jax.shard_map(
        per_device,
        mesh=mesh,
        in_specs=(P(None, "hid"), P(None, "voc"), P("hid", "voc"), P()),
        out_specs=(P("voc", "hid"), P("hid", "voc"), P("hid")),
        check_vma=False,
    )
```
